32 devices in a mesh: batch: 8 (over y, x, core), lib: 4 (over z).
Axes of the slice: x: 2, y: 2, z: 4, core: 2. Of those that a mesh axis runs over, the one named last changes fastest.
Arguments:
- skip_features: bfloat16 [64, 1024, 320], P(('batch', 'lib')), may hold values from -6 to 6
- cached_deep_features: bfloat16 [64, 1024, 640], P('lib', 'batch'), may hold values from -6 to 6
- target_position: int32 [4, 16], P('lib'), may hold values from 0 to 15, each once within a row
- request_adapter: int32 [64], P(('batch', 'lib')), may hold values from 0 to 15
- library_adapter: int32 [16], P('lib'), may hold values from 0 to 15, each once
- adapter_down_weight: bfloat16 [16, 64, 960], P('lib'), may hold values from -0.1875 to 0.1875
- adapter_up_weight: bfloat16 [16, 64, 320], P('lib'), may hold values from -0.75 to 0.75
- kernel_weight: bfloat16 [3, 3, 960, 320], replicated, may hold values from -0.0625 to 0.0625
- shortcut_matrix: bfloat16 [960, 320], replicated, may hold values from -0.1875 to 0.1875
- group_norm_gain: float32 [960], replicated, may hold values from 0.5 to 1.5
- group_norm_offset: float32 [960], replicated, may hold values from -1.8 to 1.8
- output_bias: float32 [320], replicated, may hold values from -1.8 to 1.8
Outputs:
- block_out: bfloat16 [64, 1024, 320], P(('batch', 'lib'))
The draws below stay inside these ranges and needn't reach their ends.
Inputs may be any that keep to these rules, and one draw needn't show every extreme that they name: Each row of target_position names every one of its 16 slots once. `request_adapter`: ids of adapters in the library. `library_adapter`: every adapter id is held in exactly one library slot.
All inputs are finite; a program needn't handle non-finite values.
Results may differ from the reference program's by a relative error of at most 0.0045.
Values may be sent and summed in bfloat16 or wider, within the bound.
A program may use at most 128 MiB of HBM per device.

```python
import math
import jax
import jax.numpy as jnp
import numpy as np
from jax import lax

SKIP = 320
DEEP = 640
OUTPUT_CHANNELS = 320
GROUPS = 32
ADAPTER_RANK = 64
ROWS = 32
LAT_W = 32
REQ_DEV = 2
INPUT_CHANNELS = 960
POS = 1024
COLUMN = 16
REQUESTS = 64
ADAPTER_TOTAL = 16
LIBS = 4
N_LIB = 4


def with_ends(entries, own_key, smallest, top_value):
    place = [jax.random.randint(jax.random.fold_in(own_key, axis), (), 0, length) for axis, length in enumerate(entries.shape)]
    main_axis = entries.shape.index(max(entries.shape))
    next_to = place[:main_axis] + [(place[main_axis] + 1) % entries.shape[main_axis]] + place[main_axis + 1:]
    return entries.at[tuple(place)].set(smallest).at[tuple(next_to)].set(top_value)


def levels(rng, shape, shards, least, top_value):
    loudness, own = 1.0, jax.random.fold_in(rng, 6)
    for axis_at, parts in shards:
        heights = jnp.exp(jax.random.uniform(jax.random.fold_in(own, axis_at), (parts,), jnp.float32, least / len(shards), top_value / len(shards)))
        loudness = loudness * jnp.repeat(heights, shape[axis_at] // parts).reshape([-1 if axis == axis_at else 1 for axis in range(len(shape))])
    return loudness


def cumulative_ranks(count, skew):
    loads = [(1 << 20) // math.isqrt(rank ** skew) + 1 for rank in range(1, count + 1)]
    scale = 1 + sum(loads) // (1 << 30)
    return np.cumsum(np.array([max(1, weight // scale) for weight in loads]))


def ranked_ids(rng, dims, count, lean):
    listing = cumulative_ranks(count, lean)
    lot = jax.random.randint(jax.random.fold_in(rng, 1), dims, 0, int(listing[count - 1]))
    rank = jnp.searchsorted(jnp.asarray(listing, jnp.int32), lot, side="right")
    return jax.random.permutation(jax.random.fold_in(rng, 2), count)[rank].astype(jnp.int32)


def gaussian(rng, extent, scale, bound, shards=(), kind=jnp.bfloat16):
    gain = levels(rng, extent, shards, -0.22, 0.18) if shards else 1.0
    values = jax.random.normal(rng, extent, jnp.float32) * scale * gain
    return jnp.minimum(jnp.maximum(values, -bound), bound).astype(kind)


def setup_inputs(seed: int = 0) -> dict:
    key_list = jax.random.split(jax.random.key(seed), 13)
    return {
        "skip_features": gaussian(key_list[0], (REQUESTS, POS, SKIP), 1.0, 6.0, ((0, 32),)),
        "cached_deep_features": gaussian(key_list[1], (REQUESTS, POS, DEEP), 1.0, 6.0, ((0, 4), (1, 8))),
        "target_position": jax.vmap(lambda own: jax.random.permutation(own, COLUMN))(jax.random.split(key_list[2], LIBS)).reshape((LIBS, COLUMN)).astype(jnp.int32),
        "request_adapter": with_ends(ranked_ids(key_list[3], (REQUESTS,), ADAPTER_TOTAL, 2), jax.random.fold_in(key_list[3], 3), 0, ADAPTER_TOTAL - 1).astype(jnp.int32),
        "library_adapter": jax.random.permutation(key_list[4], ADAPTER_TOTAL).astype(jnp.int32),
        "adapter_down_weight": gaussian(key_list[5], (ADAPTER_TOTAL, ADAPTER_RANK, INPUT_CHANNELS), INPUT_CHANNELS ** -0.5, 0.1875, ((0, 4),)),
        "adapter_up_weight": gaussian(key_list[6], (ADAPTER_TOTAL, ADAPTER_RANK, OUTPUT_CHANNELS), ADAPTER_RANK ** -0.5, 0.75, ((0, 4),)),
        "kernel_weight": gaussian(key_list[7], (3, 3, INPUT_CHANNELS, OUTPUT_CHANNELS), (9 * INPUT_CHANNELS) ** -0.5, 0.0625),
        "shortcut_matrix": gaussian(key_list[8], (INPUT_CHANNELS, OUTPUT_CHANNELS), INPUT_CHANNELS ** -0.5, 0.1875),
        "group_norm_gain": jnp.clip(1.0 + 0.1 * jax.random.normal(key_list[9], (INPUT_CHANNELS,), jnp.float32), 0.5, 1.5),
        "group_norm_offset": gaussian(key_list[10], (INPUT_CHANNELS,), 0.3, 1.8, (), jnp.float32),
        "output_bias": gaussian(key_list[11], (OUTPUT_CHANNELS,), 0.3, 1.8, (), jnp.float32),
    }


def norm_silu(joined, group_norm_gain, group_norm_offset):
    values = joined.astype(jnp.float32).reshape(POS, GROUPS, INPUT_CHANNELS // GROUPS)
    center = lax.optimization_barrier(jnp.mean(values, axis=(0, 2), keepdims=True))
    spread = lax.optimization_barrier(jnp.mean((values - center) ** 2, axis=(0, 2), keepdims=True))
    scaled = ((values - center) / jnp.sqrt(spread + 1e-05)).reshape(POS, INPUT_CHANNELS) * group_norm_gain + group_norm_offset
    return jax.nn.silu(scaled).astype(jnp.bfloat16)

def reference(skip_features, cached_deep_features, target_position, request_adapter, library_adapter, adapter_down_weight, adapter_up_weight, kernel_weight, shortcut_matrix, group_norm_gain, group_norm_offset, output_bias):
    lib_rows = jnp.arange(N_LIB, dtype=jnp.int32)[:, None] * jnp.ones((1, COLUMN), jnp.int32)
    slots = jnp.ones((N_LIB, 1), jnp.int32) * jnp.arange(COLUMN, dtype=jnp.int32)[None, :]
    inverse = jnp.zeros((N_LIB, COLUMN), jnp.int32).at[lib_rows, target_position].set(slots)
    holder = jnp.zeros((ADAPTER_TOTAL,), jnp.int32).at[library_adapter].set(jnp.arange(ADAPTER_TOTAL, dtype=jnp.int32))

    def one_request(index):
        lib_index = index // REQ_DEV % N_LIB
        batch_index = index // (REQ_DEV * N_LIB)
        target = batch_index * REQ_DEV + index % REQ_DEV
        source = (lib_index * COLUMN + inverse[lib_index, target]).astype(jnp.int32)
        deep = cached_deep_features[source]
        joined = jnp.concatenate([skip_features[index], deep], axis=1)
        normed = norm_silu(joined, group_norm_gain, group_norm_offset)
        padded = jnp.pad(normed.reshape(ROWS, LAT_W, INPUT_CHANNELS), ((1, 1), (1, 1), (0, 0)))
        conv = jnp.zeros((POS, OUTPUT_CHANNELS), jnp.float32)
        for row_off in range(3):
            for col_off in range(3):
                window = padded[row_off:row_off + ROWS, col_off:col_off + LAT_W].reshape(POS, INPUT_CHANNELS)
                conv = conv + jnp.dot(window, kernel_weight[row_off, col_off], preferred_element_type=jnp.float32)
        library_position = holder[request_adapter[index]]
        down_matrix = adapter_down_weight[library_position]
        up_matrix = adapter_up_weight[library_position]
        low = lax.dot_general(normed, down_matrix, (((1,), (1,)), ((), ())), preferred_element_type=jnp.float32).astype(jnp.bfloat16)
        delta = jnp.dot(low, up_matrix, preferred_element_type=jnp.float32)
        shortcut = jnp.dot(joined, shortcut_matrix, preferred_element_type=jnp.float32)
        return (shortcut + conv + output_bias + delta).astype(jnp.bfloat16)
    return lax.map(one_request, jnp.arange(REQUESTS, dtype=jnp.int32))
```

```python
import functools
import jax
import jax.numpy as jnp
import numpy as np
from jax import lax
from jax.experimental import pallas as pl
from jax.experimental.pallas import tpu as pltpu
from jax.sharding import PartitionSpec as P

GROUPS = 32
LAT_W = 32
SKIP = 320
DEEP = 640
WIDTH = SKIP + DEEP
OUT = 320
MAIN = 256
REST = OUT - MAIN
RANK = 64
CHUNK = 256
MESH = pl.DeviceIdType.MESH
PERM = ((0, 0, 256), (256, SKIP, DEEP), (256 + DEEP, 256, REST))


def same_group():
    order = np.concatenate([np.arange(s, s + n) for _, s, n in PERM])
    ids = order // (WIDTH // GROUPS)
    return (ids[:, None] == ids[None, :]).astype(np.float32)


def flip(value, mask, count):
    out, bit = 0, 1
    while bit < count:
        mine = (value // bit) % 2
        out = out + bit * ((1 - mine) if mask & bit else mine)
        bit *= 2
    return out


def move_kernel(B, L, tp, req, lib, cached, down, up, deep, dsel, usel,
                send, ids, dall, uall, s_send, s_recv, z_send, z_recv, f_send, f_recv, l_sem):
    b, l = lax.axis_index("batch"), lax.axis_index("lib")
    column, block = cached.shape[0], cached.shape[1]
    per = deep.shape[0]
    n = down.shape[0]
    h = n // 2
    half = b % 2
    peers = [flip(b, d, B) for d in range(B - 1, 0, -1)]
    zpeers = [(l + d) % L for d in range(1, L)]
    sib = peers[-1]

    barrier = pltpu.get_barrier_semaphore()
    for p in peers:
        pl.semaphore_signal(barrier, inc=1, device_id=(p, l), device_id_type=MESH)
    for z in zpeers:
        pl.semaphore_signal(barrier, inc=1, device_id=(b, z), device_id_type=MESH)
    pl.semaphore_wait(barrier, len(peers) + len(zpeers))

    def to_peer(s, p, src):
        t = p * per + s
        return pltpu.make_async_remote_copy(
            src_ref=send.at[t], dst_ref=deep.at[s, pl.ds(pl.multiple_of(src * block, block), block)],
            send_sem=s_send.at[s, p], recv_sem=s_recv.at[s, src],
            device_id=(p, l), device_id_type=MESH)

    def gather(t):
        j = jnp.int32(0)
        for i in range(column):
            j = jnp.where(tp[0, i] == t, i, j)
        send[t] = cached[j]

    def z_copies(z, src):
        part = pl.ds(half * h, h)
        row = pl.ds(src * n + half * h, h)
        kw = dict(device_id=(b, z), device_id_type=MESH)
        return [
            pltpu.make_async_remote_copy(src_ref=ids.at[src], dst_ref=ids.at[src],
                                         send_sem=z_send.at[0, z], recv_sem=z_recv.at[0, src], **kw),
            pltpu.make_async_remote_copy(src_ref=down.at[part], dst_ref=dall.at[row],
                                         send_sem=z_send.at[1, z], recv_sem=z_recv.at[1, src], **kw),
            pltpu.make_async_remote_copy(src_ref=up.at[part], dst_ref=uall.at[row],
                                         send_sem=z_send.at[2, z], recv_sem=z_recv.at[2, src], **kw),
        ]

    def f_copies(src, side):
        row = pl.ds(src * n + side * h, h)
        kw = dict(device_id=(sib, l), device_id_type=MESH)
        return [
            pltpu.make_async_remote_copy(src_ref=dall.at[row], dst_ref=dall.at[row],
                                         send_sem=f_send.at[0, src], recv_sem=f_recv.at[0, src], **kw),
            pltpu.make_async_remote_copy(src_ref=uall.at[row], dst_ref=uall.at[row],
                                         send_sem=f_send.at[1, src], recv_sem=f_recv.at[1, src], **kw),
        ]

    row_id = lax.broadcasted_iota(jnp.int32, ids.shape[1:], 0)
    mine = jnp.full(ids.shape[1:], -1, jnp.int32)
    for i in range(n):
        mine = jnp.where(row_id == i, lib[i], mine)
    ids[l] = mine
    for z in zpeers:
        for c in z_copies(z, l):
            c.start()
    own_d = pltpu.make_async_copy(down, dall.at[pl.ds(l * n, n)], l_sem.at[0])
    own_u = pltpu.make_async_copy(up, uall.at[pl.ds(l * n, n)], l_sem.at[1])
    own_d.start()
    own_u.start()
    for s in range(per):
        for p in peers:
            gather(p * per + s)
            to_peer(s, p, b).start()
    locals_ = []
    for s in range(per):
        gather(b * per + s)
        c = pltpu.make_async_copy(
            send.at[b * per + s], deep.at[s, pl.ds(pl.multiple_of(b * block, block), block)], l_sem.at[2 + s])
        c.start()
        locals_.append(c)
    for z in zpeers:
        for c in z_copies(z, z):
            c.wait_recv()
        for c in f_copies(z, half):
            c.start()
    for z in zpeers:
        for c in f_copies(z, 1 - half):
            c.wait_recv()
    own_d.wait()
    own_u.wait()
    number = lax.broadcasted_iota(jnp.int32, ids.shape, 0) * n + lax.broadcasted_iota(jnp.int32, ids.shape, 1)
    for s in range(per):
        k = jnp.max(jnp.where(ids[...] == req[s], number, 0))
        dsel[s] = dall[k]
        usel[s] = uall[k]
    for z in zpeers:
        for c in z_copies(z, l):
            c.wait_send()
        for c in f_copies(z, half):
            c.wait_send()
    for c in locals_:
        c.wait()
    for s in range(per):
        for p in peers:
            to_peer(s, p, p).wait_recv()
            to_peer(s, p, b).wait_send()


def move(B, L, tp, req, lib, cached, down, up, per, places):
    n, column, block = down.shape[0], cached.shape[0], cached.shape[1]
    vm = pl.BlockSpec(memory_space=pltpu.VMEM)
    sm = pl.BlockSpec(memory_space=pltpu.SMEM)
    dma = pltpu.SemaphoreType.DMA
    return pl.pallas_call(
        functools.partial(move_kernel, B, L),
        out_shape=(
            jax.ShapeDtypeStruct((per, places, DEEP), jnp.bfloat16),
            jax.ShapeDtypeStruct((per, RANK, WIDTH), jnp.bfloat16),
            jax.ShapeDtypeStruct((per, RANK, OUT), jnp.bfloat16),
        ),
        in_specs=[sm, sm, sm, vm, vm, vm],
        out_specs=(pl.BlockSpec(memory_space=pl.ANY), vm, vm),
        scratch_shapes=[
            pltpu.VMEM((column, block, DEEP), jnp.bfloat16),
            pltpu.VMEM((L, 8 * ((n + 7) // 8), 128), jnp.int32),
            pltpu.VMEM((L * n, RANK, WIDTH), jnp.bfloat16),
            pltpu.VMEM((L * n, RANK, OUT), jnp.bfloat16),
            dma((per, B)), dma((per, B)), dma((3, L)), dma((3, L)), dma((2, L)), dma((2, L)), dma((2 + per,)),
        ],
        compiler_params=pltpu.CompilerParams(
            collective_id=0, has_side_effects=True, vmem_limit_bytes=40 * 1024 * 1024),
    )(tp, req, lib, cached, down, up)


def build_weights(kw, w):
    for dc in range(3):
        for dst, src, n in PERM:
            rows, at = slice(src, src + n), slice(dst, dst + n)
            for dr in range(3):
                w[dc, at, dr * MAIN:(dr + 1) * MAIN] = kw[dr, dc, rows, :MAIN]
            w[dc, at, 768:896] = jnp.concatenate([kw[0, dc, rows, MAIN:], kw[1, dc, rows, MAIN:]], axis=1)
            w[dc, at, 896:1024] = jnp.concatenate(
                [kw[2, dc, rows, MAIN:], jnp.zeros((n, RANK), jnp.bfloat16)], axis=1)


def permuted(ref):
    return jnp.concatenate([ref[:, s:s + n] for _, s, n in PERM], axis=1)


def group_sum(v, same):
    v = jnp.sum(v, axis=0, keepdims=True)
    hi = v.astype(jnp.bfloat16).astype(jnp.float32)
    mid = (v - hi).astype(jnp.bfloat16).astype(jnp.float32)
    lo = v - hi - mid
    r = lax.broadcasted_iota(jnp.int32, (16, v.shape[1]), 0)
    rows = jnp.where(r == 0, hi, jnp.where(r == 1, mid, jnp.where(r == 2, lo, 0.0))).astype(jnp.bfloat16)
    return jnp.sum(jnp.dot(rows, same, preferred_element_type=jnp.float32), axis=0, keepdims=True)


def load_joined(skip, deep, at):
    sk = skip[0, at, :].astype(jnp.float32)
    return jnp.concatenate([sk[:, :256], deep[0, at, :].astype(jnp.float32), sk[:, 256:]], axis=1)


def block_kernel(skip, deep, dsel, usel, kw, sc, gain, offset, bias, same, out, w, x, acc):
    places = skip.shape[1]
    count = places * (WIDTH // GROUPS)

    @pl.when(pl.program_id(0) == 0)
    def _():
        build_weights(kw, w)

    dt = dsel[0].astype(jnp.float32).T.astype(jnp.bfloat16)
    for dst, src, n in PERM:
        w[1, dst:dst + n, 896:1024] = jnp.concatenate([kw[2, 1, src:src + n, MAIN:], dt[src:src + n]], axis=1)

    step = 64

    def total(i, c):
        v = load_joined(skip, deep, pl.ds(pl.multiple_of(i * step, step), step))
        return c + jnp.sum(v.reshape(step // 8, 8, WIDTH), axis=0)

    zero = jnp.zeros((8, WIDTH), jnp.float32)
    mean = group_sum(lax.fori_loop(0, places // step, total, zero), same[...]) * (1.0 / count)

    def square(i, c):
        v = load_joined(skip, deep, pl.ds(pl.multiple_of(i * step, step), step)) - mean
        return c + jnp.sum((v * v).reshape(step // 8, 8, WIDTH), axis=0)

    var = group_sum(lax.fori_loop(0, places // step, square, zero), same[...]) * (1.0 / count)
    scale = 0.5 * permuted(gain) * lax.rsqrt(var + 1e-5)
    shift = 0.5 * permuted(offset)

    def normed(i, c):
        at = pl.ds(pl.multiple_of(i * step, step), step)
        z = (load_joined(skip, deep, at) - mean) * scale + shift
        x[at, :] = (z + z * jnp.tanh(z)).astype(jnp.bfloat16)
        return c

    lax.fori_loop(0, places // step, normed, 0)

    def shortcut(i, c):
        p = pl.multiple_of(i * CHUNK, CHUNK)
        at = pl.ds(p, CHUNK)
        acc[pl.ds(p + LAT_W, CHUNK), :] = (
            jnp.dot(skip[0, at, :], sc[:SKIP, :], preferred_element_type=jnp.float32)
            + jnp.dot(deep[0, at, :], sc[SKIP:, :], preferred_element_type=jnp.float32)
            + bias[...]
        )
        return c

    lax.fori_loop(0, places // CHUNK, shortcut, 0)
    edge = jnp.zeros((LAT_W, OUT), jnp.float32)
    acc[:LAT_W, :] = edge
    acc[places + LAT_W:, :] = edge

    def conv(i, c):
        p = pl.multiple_of(i * CHUNK, CHUNK)
        xs = x[pl.ds(p, CHUNK), :]
        col = lax.broadcasted_iota(jnp.int32, (CHUNK, 1), 0) % LAT_W
        y1 = jnp.dot(xs, w[1], preferred_element_type=jnp.float32)
        y0 = jnp.dot(xs, w[0], preferred_element_type=jnp.float32)
        v = y1 + jnp.where(col != 0, pltpu.roll(y0, 1, 0), 0.0)
        y2 = jnp.dot(xs, w[2], preferred_element_type=jnp.float32)
        v = v + jnp.where(col != LAT_W - 1, pltpu.roll(y2, CHUNK - 1, 0), 0.0)
        low = y1[:, 3 * OUT:].astype(jnp.bfloat16)
        delta = jnp.dot(low, usel[0], preferred_element_type=jnp.float32)
        for dr in range(3):
            at = pl.ds(pl.multiple_of(p + (2 - dr) * LAT_W, LAT_W), CHUNK)
            a = v[:, dr * MAIN:(dr + 1) * MAIN]
            e = v[:, 3 * MAIN + dr * REST:3 * MAIN + (dr + 1) * REST]
            if dr == 1:
                a, e = a + delta[:, :MAIN], e + delta[:, MAIN:]
            acc[at, :MAIN] += a
            acc[at, MAIN:] += e
        return c

    lax.fori_loop(0, places // CHUNK, conv, 0)
    out[0] = acc[pl.ds(LAT_W, places), :].astype(jnp.bfloat16)


def compute(skip, deep, dsel, usel, kw, sc, gain, offset, bias):
    per, places = skip.shape[0], skip.shape[1]
    same = jnp.asarray(same_group(), jnp.bfloat16)
    vm = pl.BlockSpec(memory_space=pltpu.VMEM)

    def one(a):
        return pl.BlockSpec((1,) + a.shape[1:], lambda r: (r, 0, 0))

    return pl.pallas_call(
        block_kernel,
        grid=(per,),
        out_shape=jax.ShapeDtypeStruct((per, places, OUT), jnp.bfloat16),
        in_specs=[one(skip), one(deep), one(dsel), one(usel), vm, vm, vm, vm, vm, vm],
        out_specs=pl.BlockSpec((1, places, OUT), lambda r: (r, 0, 0)),
        scratch_shapes=[
            pltpu.VMEM((3, WIDTH, 1024), jnp.bfloat16),
            pltpu.VMEM((places, WIDTH), jnp.bfloat16),
            pltpu.VMEM((places + 2 * LAT_W, OUT), jnp.float32),
        ],
        compiler_params=pltpu.CompilerParams(vmem_limit_bytes=56 * 1024 * 1024),
    )(skip, deep, dsel, usel, kw, sc, gain[None], offset[None], bias[None], same)


def solution(mesh):
    B, L = mesh.shape["batch"], mesh.shape["lib"]

    def local(skip, cached, tp, req, lib, down, up, kw, sc, gain, offset, bias):
        per, places = skip.shape[0], skip.shape[1]
        deep, dsel, usel = move(B, L, tp, req, lib, cached, down, up, per, places)
        return compute(skip, deep, dsel, usel, kw, sc, gain, offset, bias)

    both = P(("batch", "lib"), None, None)
    lib3 = P("lib", None, None)
    in_specs = (both, P("lib", "batch", None), P("lib", None), P(("batch", "lib")), P("lib"), lib3, lib3,
                P(), P(), P(), P(), P())
    return jax.shard_map(local, mesh=mesh, in_specs=in_specs, out_specs=both, check_vma=False)
```

```python
import functools
import jax
import jax.numpy as jnp
import numpy as np
from jax import lax
from jax.experimental import pallas as pl
from jax.experimental.pallas import tpu as pltpu
from jax.sharding import PartitionSpec as P

GROUPS = 32
LAT_W = 32
SKIP = 320
DEEP = 640
WIDTH = SKIP + DEEP
OUT = 320
MAIN = 256
REST = OUT - MAIN
RANK = 64
CHUNK = 256
MESH = pl.DeviceIdType.MESH
def same_group():
    ids = np.arange(WIDTH) // (WIDTH // GROUPS)
    return (ids[:, None] == ids[None, :]).astype(np.float32)


def dot_t(a, b):
    return lax.dot_general(a, b, (((1,), (1,)), ((), ())), preferred_element_type=jnp.float32)


def flip(value, mask, count):
    out, bit = 0, 1
    while bit < count:
        mine = (value // bit) % 2
        out = out + bit * ((1 - mine) if mask & bit else mine)
        bit *= 2
    return out


def group_sum(v, same):
    v = jnp.sum(v, axis=0, keepdims=True)
    hi = v.astype(jnp.bfloat16).astype(jnp.float32)
    mid = (v - hi).astype(jnp.bfloat16).astype(jnp.float32)
    lo = v - hi - mid
    r = lax.broadcasted_iota(jnp.int32, (16, v.shape[1]), 0)
    rows = jnp.where(r == 0, hi, jnp.where(r == 1, mid, jnp.where(r == 2, lo, 0.0))).astype(jnp.bfloat16)
    return jnp.sum(jnp.dot(rows, same, preferred_element_type=jnp.float32), axis=0, keepdims=True)


def kernel(B, L, tp, req, lib, cached_h, down, up, skip_h, kw_h, sc_h, gain, offset, bias, same_h, out,
           cached, send, deep, ids, dall, uall, w, sc, skip_t, skip, x, y, acc, same,
           s_send, s_recv, z_send, z_recv, f_send, f_recv, l_sem, w_sem):
    b, l = lax.axis_index("batch"), lax.axis_index("lib")
    column, block = cached.shape[0], cached.shape[1]
    per, places = deep.shape[0], deep.shape[1]
    n = down.shape[0]
    h = n // 2
    half = b % 2
    peers = [flip(b, d, B) for d in range(B - 1, 0, -1)]
    zpeers = [(l + d) % L for d in range(1, L)]
    sib = peers[-1]

    load_cached = pltpu.make_async_copy(cached_h, cached, l_sem.at[0])
    load_cached.start()
    loads = [
        pltpu.make_async_copy(skip_h, skip_t, l_sem.at[1]),
        pltpu.make_async_copy(sc_h, sc, l_sem.at[2]),
        pltpu.make_async_copy(same_h, same, l_sem.at[3]),
    ]
    w_loads = []
    for dr in range(3):
        for dc in range(3):
            i = 2 * (3 * dr + dc)
            w_loads.append(pltpu.make_async_copy(
                kw_h.at[dr, dc, pl.ds(0, MAIN)], w.at[dc, pl.ds(dr * MAIN, MAIN)], w_sem.at[i]))
            w_loads.append(pltpu.make_async_copy(
                kw_h.at[dr, dc, pl.ds(MAIN, REST)], w.at[dc, pl.ds(3 * MAIN + dr * REST, REST)], w_sem.at[i + 1]))

    barrier = pltpu.get_barrier_semaphore()
    for p in peers:
        pl.semaphore_signal(barrier, inc=1, device_id=(p, l), device_id_type=MESH)
    for z in zpeers:
        pl.semaphore_signal(barrier, inc=1, device_id=(b, z), device_id_type=MESH)
    pl.semaphore_wait(barrier, len(peers) + len(zpeers))

    def to_peer(s, p, src):
        return pltpu.make_async_remote_copy(
            src_ref=send.at[p * per + s], dst_ref=deep.at[s, pl.ds(pl.multiple_of(src * block, block), block)],
            send_sem=s_send.at[s, p], recv_sem=s_recv.at[s, src],
            device_id=(p, l), device_id_type=MESH)

    def slot(t):
        j = jnp.int32(0)
        for i in range(column):
            j = jnp.where(tp[0, i] == t, i, j)
        return j

    def z_copies(z, src):
        part = pl.ds(half * h, h)
        row = pl.ds(src * n + half * h, h)
        kw = dict(device_id=(b, z), device_id_type=MESH)
        return [
            pltpu.make_async_remote_copy(src_ref=ids.at[src], dst_ref=ids.at[src],
                                         send_sem=z_send.at[0, z], recv_sem=z_recv.at[0, src], **kw),
            pltpu.make_async_remote_copy(src_ref=down.at[part], dst_ref=dall.at[row],
                                         send_sem=z_send.at[1, z], recv_sem=z_recv.at[1, src], **kw),
            pltpu.make_async_remote_copy(src_ref=up.at[part], dst_ref=uall.at[row],
                                         send_sem=z_send.at[2, z], recv_sem=z_recv.at[2, src], **kw),
        ]

    def f_copies(src, side):
        row = pl.ds(src * n + side * h, h)
        kw = dict(device_id=(sib, l), device_id_type=MESH)
        return [
            pltpu.make_async_remote_copy(src_ref=dall.at[row], dst_ref=dall.at[row],
                                         send_sem=f_send.at[0, src], recv_sem=f_recv.at[0, src], **kw),
            pltpu.make_async_remote_copy(src_ref=uall.at[row], dst_ref=uall.at[row],
                                         send_sem=f_send.at[1, src], recv_sem=f_recv.at[1, src], **kw),
        ]

    load_cached.wait()
    for s in range(per):
        for p in peers:
            send[p * per + s] = cached[slot(p * per + s)]
            to_peer(s, p, b).start()
        if s == 0:
            row_id = lax.broadcasted_iota(jnp.int32, ids.shape[1:], 0)
            mine = jnp.full(ids.shape[1:], -1, jnp.int32)
            for i in range(n):
                mine = jnp.where(row_id == i, lib[i], mine)
            ids[l] = mine
            for z in zpeers:
                for c in z_copies(z, l):
                    c.start()
    for c in loads + w_loads:
        c.start()
    for s in range(per):
        deep[s, pl.ds(pl.multiple_of(b * block, block), block), :] = cached[slot(b * per + s)]
    dall[pl.ds(l * n, n)] = down[...]
    uall[pl.ds(l * n, n)] = up[...]
    edge = jnp.zeros((3, LAT_W, 1024), jnp.float32)
    y[:, :LAT_W, :] = edge
    y[:, places + LAT_W:, :] = edge
    for c in loads:
        c.wait()

    for s in range(per):
        for i in range(places // CHUNK):
            at = pl.ds(i * CHUNK, CHUNK)
            sk = skip_t[s, :, at].astype(jnp.float32).T.astype(jnp.bfloat16)
            skip[s, at, :] = sk
            acc[s, at, :] = dot_t(sk, sc[:, :SKIP]) + bias[...]

    for z in zpeers:
        for c in z_copies(z, z):
            c.wait_recv()
        for c in f_copies(z, half):
            c.start()
    for z in zpeers:
        for c in f_copies(z, 1 - half):
            c.wait_recv()
    for c in w_loads:
        c.wait()
    number = lax.broadcasted_iota(jnp.int32, ids.shape, 0) * n + lax.broadcasted_iota(jnp.int32, ids.shape, 1)
    count = places * (WIDTH // GROUPS)
    step = 64

    def request(s, carry):
        k = jnp.max(jnp.where(ids[...] == req[s], number, 0))
        w[1, 3 * OUT:, :] = dall[k]
        u = uall[k]
        for p in peers:
            to_peer(s, p, p).wait_recv()

        def both(i):
            at = pl.ds(pl.multiple_of(i * step, step), step)
            return skip[s, at, :].astype(jnp.float32), deep[s, at, :].astype(jnp.float32)

        def fold(v):
            return jnp.sum(v.reshape(step // 8, 8, v.shape[1]), axis=0)

        def total(i, c):
            a, d = both(i)
            return c[0] + fold(a), c[1] + fold(d)

        zero = (jnp.zeros((8, SKIP), jnp.float32), jnp.zeros((8, DEEP), jnp.float32))
        t = lax.fori_loop(0, places // step, total, zero)
        mean = group_sum(jnp.concatenate(t, axis=1), same[...]) * (1.0 / count)
        mean_s, mean_d = mean[:, :SKIP], mean[:, SKIP:]

        def square(i, c):
            a, d = both(i)
            a, d = a - mean_s, d - mean_d
            return c[0] + fold(a * a), c[1] + fold(d * d)

        t = lax.fori_loop(0, places // step, square, zero)
        var = group_sum(jnp.concatenate(t, axis=1), same[...]) * (1.0 / count)
        scale = 0.5 * gain[...] * lax.rsqrt(var + 1e-5)
        shift = 0.5 * offset[...]
        scale_s, scale_d = scale[:, :SKIP], scale[:, SKIP:]
        shift_s, shift_d = shift[:, :SKIP], shift[:, SKIP:]

        def normed(i, c):
            a, d = both(i)
            a = (a - mean_s) * scale_s + shift_s
            d = (d - mean_d) * scale_d + shift_d
            a = (a + a * jnp.tanh(a)).astype(jnp.bfloat16)
            d = (d + d * jnp.tanh(d)).astype(jnp.bfloat16)
            x[pl.ds(pl.multiple_of(i * step, step), step), :] = jnp.concatenate([a, d], axis=1)
            return c

        lax.fori_loop(0, places // step, normed, 0)

        def conv(i, c):
            p = pl.multiple_of(i * CHUNK, CHUNK)
            at = pl.ds(p, CHUNK)
            xs = x[at, :]
            to = pl.ds(pl.multiple_of(p + LAT_W, LAT_W), CHUNK)
            y1 = dot_t(xs, w[1])
            y[1, to, :] = y1
            y[0, to, :3 * OUT] = dot_t(xs, w[0, :3 * OUT])
            y[2, to, :3 * OUT] = dot_t(xs, w[2, :3 * OUT])
            acc[s, at, :] += (
                dot_t(deep[s, at, :], sc[:, SKIP:])
                + jnp.dot(y1[:, 3 * OUT:].astype(jnp.bfloat16), u, preferred_element_type=jnp.float32)
            )
            return c

        lax.fori_loop(0, places // CHUNK, conv, 0)
        side = 128

        def gather_taps(i, c):
            p = pl.multiple_of(i * side, side)
            col = lax.broadcasted_iota(jnp.int32, (side, 1), 0) % LAT_W

            def rows(dc, dr, lo, size):
                return y[dc, pl.ds(pl.multiple_of(p + dr * LAT_W, LAT_W), side), lo:lo + size]

            def column_sum(dc):
                a = rows(dc, 0, 0, MAIN) + rows(dc, 1, MAIN, MAIN) + rows(dc, 2, 2 * MAIN, MAIN)
                e = (rows(dc, 0, 3 * MAIN, 128) + rows(dc, 2, 3 * MAIN + 128, 128))[:, :REST]
                e = e + rows(dc, 1, 3 * MAIN, 128)[:, REST:]
                return jnp.concatenate([a, e], axis=1)

            v = column_sum(1) + acc[s, pl.ds(p, side), :]
            v = v + jnp.where(col != 0, pltpu.roll(column_sum(0), 1, 0), 0.0)
            v = v + jnp.where(col != LAT_W - 1, pltpu.roll(column_sum(2), side - 1, 0), 0.0)
            out[s, :, pl.ds(p, side)] = v.T.astype(jnp.bfloat16)
            return c

        lax.fori_loop(0, places // side, gather_taps, 0)
        return carry

    lax.fori_loop(0, per, request, 0)
    for z in zpeers:
        for c in z_copies(z, l):
            c.wait_send()
        for c in f_copies(z, half):
            c.wait_send()
    for s in range(per):
        for p in peers:
            to_peer(s, p, b).wait_send()


def solution(mesh):
    B, L = mesh.shape["batch"], mesh.shape["lib"]

    def local(skip, cached, tp, req, lib, down, up, kw, sc, gain, offset, bias):
        per, places = skip.shape[0], skip.shape[1]
        n, column, block = down.shape[0], cached.shape[0], cached.shape[1]
        vm = pl.BlockSpec(memory_space=pltpu.VMEM)
        sm = pl.BlockSpec(memory_space=pltpu.SMEM)
        hbm = pl.BlockSpec(memory_space=pl.ANY)
        dma = pltpu.SemaphoreType.DMA
        bf, f32 = jnp.bfloat16, jnp.float32
        out = pl.pallas_call(
            functools.partial(kernel, B, L),
            out_shape=jax.ShapeDtypeStruct((per, OUT, places), bf),
            in_specs=[sm, sm, sm, hbm, vm, vm, hbm, hbm, hbm, vm, vm, vm, hbm],
            out_specs=vm,
            scratch_shapes=[
                pltpu.VMEM((column, block, DEEP), bf),
                pltpu.VMEM((column, block, DEEP), bf),
                pltpu.VMEM((per, places, DEEP), bf),
                pltpu.VMEM((L, 8 * ((n + 7) // 8), 128), jnp.int32),
                pltpu.VMEM((L * n, RANK, WIDTH), bf),
                pltpu.VMEM((L * n, RANK, OUT), bf),
                pltpu.VMEM((3, 1024, WIDTH), bf),
                pltpu.VMEM((OUT, WIDTH), bf),
                pltpu.VMEM((per, SKIP, places), bf),
                pltpu.VMEM((per, places, SKIP), bf),
                pltpu.VMEM((places, WIDTH), bf),
                pltpu.VMEM((3, places + 2 * LAT_W, 1024), f32),
                pltpu.VMEM((per, places, OUT), f32),
                pltpu.VMEM((WIDTH, WIDTH), bf),
                dma((per, B)), dma((per, B)), dma((3, L)), dma((3, L)), dma((2, L)), dma((2, L)), dma((4,)),
                dma((18,)),
            ],
            compiler_params=pltpu.CompilerParams(
                collective_id=0, has_side_effects=True, vmem_limit_bytes=60 * 1024 * 1024),
        )(tp, req, lib, cached, down, up, skip.transpose(0, 2, 1), kw.transpose(0, 1, 3, 2), sc.T,
          gain[None], offset[None], bias[None], jnp.asarray(same_group(), bf))
        return out.transpose(0, 2, 1)

    both = P(("batch", "lib"), None, None)
    lib3 = P("lib", None, None)
    in_specs = (both, P("lib", "batch", None), P("lib", None), P(("batch", "lib")), P("lib"), lib3, lib3,
                P(), P(), P(), P(), P())
    return jax.shard_map(local, mesh=mesh, in_specs=in_specs, out_specs=both, check_vma=False)
```

```python
import functools
import jax
import jax.numpy as jnp
import numpy as np
from jax import lax
from jax.experimental import pallas as pl
from jax.experimental.pallas import tpu as pltpu
from jax.sharding import PartitionSpec as P

GROUPS = 32
LAT_W = 32
SKIP = 320
DEEP = 640
WIDTH = SKIP + DEEP
OUT = 320
MAIN = 256
REST = OUT - MAIN
RANK = 64
CHUNK = 256
MESH = pl.DeviceIdType.MESH
def same_group():
    ids = np.arange(WIDTH) // (WIDTH // GROUPS)
    return (ids[:, None] == ids[None, :]).astype(np.float32)


def dot_t(a, b):
    return lax.dot_general(a, b, (((1,), (1,)), ((), ())), preferred_element_type=jnp.float32)


def flip(value, mask, count):
    out, bit = 0, 1
    while bit < count:
        mine = (value // bit) % 2
        out = out + bit * ((1 - mine) if mask & bit else mine)
        bit *= 2
    return out


def group_sum(v, same):
    v = jnp.sum(v, axis=0, keepdims=True)
    hi = v.astype(jnp.bfloat16).astype(jnp.float32)
    mid = (v - hi).astype(jnp.bfloat16).astype(jnp.float32)
    lo = v - hi - mid
    r = lax.broadcasted_iota(jnp.int32, (16, v.shape[1]), 0)
    rows = jnp.where(r == 0, hi, jnp.where(r == 1, mid, jnp.where(r == 2, lo, 0.0))).astype(jnp.bfloat16)
    return jnp.sum(jnp.dot(rows, same, preferred_element_type=jnp.float32), axis=0, keepdims=True)


def kernel(B, L, tp, req, lib, cached_h, down, up, skip_h, kw_h, sc_h, gain, offset, bias, same_h, out,
           cached, send, deep, ids, dall, uall, w, sc, skip_t, skip, x, y, acc, same,
           s_send, s_recv, z_send, z_recv, f_send, f_recv, l_sem, w_sem):
    b, l = lax.axis_index("batch"), lax.axis_index("lib")
    column, block = cached.shape[0], cached.shape[1]
    per, places = deep.shape[0], deep.shape[1]
    n = down.shape[0]
    h = n // 2
    half = b % 2
    peers = [flip(b, d, B) for d in range(B - 1, 0, -1)]
    zpeers = [(l + d) % L for d in range(1, L)]
    sib = peers[-1]

    load_cached = pltpu.make_async_copy(cached_h, cached, l_sem.at[0])
    load_cached.start()
    loads = [
        pltpu.make_async_copy(skip_h, skip_t, l_sem.at[1]),
        pltpu.make_async_copy(sc_h, sc, l_sem.at[2]),
        pltpu.make_async_copy(same_h, same, l_sem.at[3]),
    ]
    w_loads = []
    for dr in range(3):
        for dc in range(3):
            i = 2 * (3 * dr + dc)
            w_loads.append(pltpu.make_async_copy(
                kw_h.at[dr, dc, pl.ds(0, MAIN)], w.at[dc, pl.ds(dr * MAIN, MAIN)], w_sem.at[i]))
            w_loads.append(pltpu.make_async_copy(
                kw_h.at[dr, dc, pl.ds(MAIN, REST)], w.at[dc, pl.ds(3 * MAIN + dr * REST, REST)], w_sem.at[i + 1]))

    barrier = pltpu.get_barrier_semaphore()
    for p in peers:
        pl.semaphore_signal(barrier, inc=1, device_id=(p, l), device_id_type=MESH)
    for z in zpeers:
        pl.semaphore_signal(barrier, inc=1, device_id=(b, z), device_id_type=MESH)
    pl.semaphore_wait(barrier, len(peers) + len(zpeers))

    def to_peer(s, p, src):
        return pltpu.make_async_remote_copy(
            src_ref=send.at[p * per + s], dst_ref=deep.at[s, pl.ds(pl.multiple_of(src * block, block), block)],
            send_sem=s_send.at[s, p], recv_sem=s_recv.at[s, src],
            device_id=(p, l), device_id_type=MESH)

    def slot(t):
        j = jnp.int32(0)
        for i in range(column):
            j = jnp.where(tp[0, i] == t, i, j)
        return j

    def inside(v):
        return jnp.logical_and(v >= 0, v < L)

    def z_copies(way, src):
        row = pl.ds(src * n + half * h, h)
        kw = dict(device_id=(b, (l + way + L) % L), device_id_type=MESH)
        return [
            pltpu.make_async_remote_copy(src_ref=ref, dst_ref=ref, send_sem=z_send.at[i, (way + 1) // 2, src],
                                         recv_sem=z_recv.at[i, src], **kw)
            for i, ref in enumerate((ids.at[src], dall.at[row], uall.at[row]))
        ]

    def pass_on(way, src, done=False):
        @pl.when(inside(l + way))
        def _():
            for c in z_copies(way, src):
                c.wait_send() if done else c.start()

    def f_copies(src, side):
        row = pl.ds(src * n + side * h, h)
        kw = dict(device_id=(sib, l), device_id_type=MESH)
        return [
            pltpu.make_async_remote_copy(src_ref=dall.at[row], dst_ref=dall.at[row],
                                         send_sem=f_send.at[0, src], recv_sem=f_recv.at[0, src], **kw),
            pltpu.make_async_remote_copy(src_ref=uall.at[row], dst_ref=uall.at[row],
                                         send_sem=f_send.at[1, src], recv_sem=f_recv.at[1, src], **kw),
        ]

    def z_step(d):
        for way in (1, -1):
            src = l - way * d

            @pl.when(inside(src))
            def _():
                for c in z_copies(way, src):
                    c.wait_recv()
                pass_on(way, src)
                for c in f_copies(src, half):
                    c.start()

    def z_sent(d):
        for way in (1, -1):
            src = l - way * d

            @pl.when(inside(src))
            def _():
                pass_on(way, src, done=True)

    dall[pl.ds(l * n, n)] = down[...]
    uall[pl.ds(l * n, n)] = up[...]
    load_cached.wait()
    for s in range(per):
        for p in peers:
            send[p * per + s] = cached[slot(p * per + s)]
            if s == 0:
                to_peer(s, p, b).start()
        if s == 0:
            row_id = lax.broadcasted_iota(jnp.int32, ids.shape[1:], 0)
            mine = jnp.full(ids.shape[1:], -1, jnp.int32)
            for i in range(n):
                mine = jnp.where(row_id == i, lib[i], mine)
            ids[l] = mine
            for way in (1, -1):
                pass_on(way, l)
    for c in loads + w_loads:
        c.start()
    for s in range(per):
        deep[s, pl.ds(pl.multiple_of(b * block, block), block), :] = cached[slot(b * per + s)]
    edge = jnp.zeros((3, LAT_W, 1024), jnp.float32)
    y[:, :LAT_W, :] = edge
    y[:, places + LAT_W:, :] = edge
    for c in loads:
        c.wait()

    for s in range(per):
        for i in range(places // CHUNK):
            at = pl.ds(i * CHUNK, CHUNK)
            sk = skip_t[s, :, at].astype(jnp.float32).T.astype(jnp.bfloat16)
            skip[s, at, :] = sk
            acc[s, at, :] = dot_t(sk, sc[:, :SKIP]) + bias[...]
        if s + 1 < L - 1:
            z_step(s + 1)

    for s in range(1, per):
        for p in peers:
            to_peer(s - 1, p, b).wait_send()
            to_peer(s, p, b).start()
    for d in range(min(per, L - 2) + 1, L):
        z_step(d)
    for z in zpeers:
        for c in f_copies(z, 1 - half):
            c.wait_recv()
    for c in w_loads:
        c.wait()
    number = lax.broadcasted_iota(jnp.int32, ids.shape, 0) * n + lax.broadcasted_iota(jnp.int32, ids.shape, 1)
    count = places * (WIDTH // GROUPS)
    step = 256

    def request(s, carry):
        k = jnp.max(jnp.where(ids[...] == req[s], number, 0))
        w[1, 3 * OUT:, :] = dall[k]
        u = uall[k]
        for p in peers:
            to_peer(s, p, p).wait_recv()

        def both(i):
            at = pl.ds(pl.multiple_of(i * step, step), step)
            return skip[s, at, :].astype(jnp.float32), deep[s, at, :].astype(jnp.float32)

        def fold(v):
            return jnp.sum(v.reshape(step // 8, 8, v.shape[1]), axis=0)

        def total(i, c):
            a, d = both(i)
            return c[0] + fold(a), c[1] + fold(d)

        zero = (jnp.zeros((8, SKIP), jnp.float32), jnp.zeros((8, DEEP), jnp.float32))
        t = lax.fori_loop(0, places // step, total, zero)
        mean = group_sum(jnp.concatenate(t, axis=1), same[...]) * (1.0 / count)
        mean_s, mean_d = mean[:, :SKIP], mean[:, SKIP:]

        def square(i, c):
            a, d = both(i)
            a, d = a - mean_s, d - mean_d
            return c[0] + fold(a * a), c[1] + fold(d * d)

        t = lax.fori_loop(0, places // step, square, zero)
        var = group_sum(jnp.concatenate(t, axis=1), same[...]) * (1.0 / count)
        scale = 0.5 * gain[...] * lax.rsqrt(var + 1e-5)
        shift = 0.5 * offset[...]
        scale_s, scale_d = scale[:, :SKIP], scale[:, SKIP:]
        shift_s, shift_d = shift[:, :SKIP], shift[:, SKIP:]

        def normed(i, c):
            a, d = both(i)
            a = (a - mean_s) * scale_s + shift_s
            d = (d - mean_d) * scale_d + shift_d
            a = (a + a * jnp.tanh(a)).astype(jnp.bfloat16)
            d = (d + d * jnp.tanh(d)).astype(jnp.bfloat16)
            x[pl.ds(pl.multiple_of(i * step, step), step), :] = jnp.concatenate([a, d], axis=1)
            return c

        lax.fori_loop(0, places // step, normed, 0)

        def conv(i, c):
            p = pl.multiple_of(i * CHUNK, CHUNK)
            at = pl.ds(p, CHUNK)
            xs = x[at, :]
            to = pl.ds(pl.multiple_of(p + LAT_W, LAT_W), CHUNK)
            y1 = dot_t(xs, w[1])
            y[1, to, :] = y1
            y[0, to, :3 * OUT] = dot_t(xs, w[0, :3 * OUT])
            y[2, to, :3 * OUT] = dot_t(xs, w[2, :3 * OUT])
            acc[s, at, :] += (
                dot_t(deep[s, at, :], sc[:, SKIP:])
                + jnp.dot(y1[:, 3 * OUT:].astype(jnp.bfloat16), u, preferred_element_type=jnp.float32)
            )
            return c

        lax.fori_loop(0, places // CHUNK, conv, 0)
        side = 128

        def gather_taps(i, c):
            p = pl.multiple_of(i * side, side)
            col = lax.broadcasted_iota(jnp.int32, (side, 1), 0) % LAT_W

            def rows(dc, dr, lo, size):
                return y[dc, pl.ds(pl.multiple_of(p + dr * LAT_W, LAT_W), side), lo:lo + size]

            def column_sum(dc):
                a = rows(dc, 0, 0, MAIN) + rows(dc, 1, MAIN, MAIN) + rows(dc, 2, 2 * MAIN, MAIN)
                e = (rows(dc, 0, 3 * MAIN, 128) + rows(dc, 2, 3 * MAIN + 128, 128))[:, :REST]
                e = e + rows(dc, 1, 3 * MAIN, 128)[:, REST:]
                return jnp.concatenate([a, e], axis=1)

            v = column_sum(1) + acc[s, pl.ds(p, side), :]
            v = v + jnp.where(col != 0, pltpu.roll(column_sum(0), 1, 0), 0.0)
            v = v + jnp.where(col != LAT_W - 1, pltpu.roll(column_sum(2), side - 1, 0), 0.0)
            out[s, :, pl.ds(p, side)] = v.T.astype(jnp.bfloat16)
            return c

        lax.fori_loop(0, places // side, gather_taps, 0)
        return carry

    lax.fori_loop(0, per, request, 0)
    for d in range(L):
        z_sent(d)
    for z in zpeers:
        for c in f_copies(z, half):
            c.wait_send()
    for p in peers:
        to_peer(per - 1, p, b).wait_send()


def solution(mesh):
    B, L = mesh.shape["batch"], mesh.shape["lib"]

    def local(skip, cached, tp, req, lib, down, up, kw, sc, gain, offset, bias):
        per, places = skip.shape[0], skip.shape[1]
        n, column, block = down.shape[0], cached.shape[0], cached.shape[1]
        vm = pl.BlockSpec(memory_space=pltpu.VMEM)
        sm = pl.BlockSpec(memory_space=pltpu.SMEM)
        hbm = pl.BlockSpec(memory_space=pl.ANY)
        dma = pltpu.SemaphoreType.DMA
        bf, f32 = jnp.bfloat16, jnp.float32
        out = pl.pallas_call(
            functools.partial(kernel, B, L),
            out_shape=jax.ShapeDtypeStruct((per, OUT, places), bf),
            in_specs=[sm, sm, sm, hbm, vm, vm, hbm, hbm, hbm, vm, vm, vm, hbm],
            out_specs=vm,
            scratch_shapes=[
                pltpu.VMEM((column, block, DEEP), bf),
                pltpu.VMEM((column, block, DEEP), bf),
                pltpu.VMEM((per, places, DEEP), bf),
                pltpu.VMEM((L, 8 * ((n + 7) // 8), 128), jnp.int32),
                pltpu.VMEM((L * n, RANK, WIDTH), bf),
                pltpu.VMEM((L * n, RANK, OUT), bf),
                pltpu.VMEM((3, 1024, WIDTH), bf),
                pltpu.VMEM((OUT, WIDTH), bf),
                pltpu.VMEM((per, SKIP, places), bf),
                pltpu.VMEM((per, places, SKIP), bf),
                pltpu.VMEM((places, WIDTH), bf),
                pltpu.VMEM((3, places + 2 * LAT_W, 1024), f32),
                pltpu.VMEM((per, places, OUT), f32),
                pltpu.VMEM((WIDTH, WIDTH), bf),
                dma((per, B)), dma((per, B)), dma((3, 2, L)), dma((3, L)), dma((2, L)), dma((2, L)), dma((4,)),
                dma((18,)),
            ],
            compiler_params=pltpu.CompilerParams(
                collective_id=0, has_side_effects=True, vmem_limit_bytes=60 * 1024 * 1024),
        )(tp, req, lib, cached, down, up, skip.transpose(0, 2, 1), kw.transpose(0, 1, 3, 2), sc.T,
          gain[None], offset[None], bias[None], jnp.asarray(same_group(), bf))
        return out.transpose(0, 2, 1)

    both = P(("batch", "lib"), None, None)
    lib3 = P("lib", None, None)
    in_specs = (both, P("lib", "batch", None), P("lib", None), P(("batch", "lib")), P("lib"), lib3, lib3,
                P(), P(), P(), P(), P())
    return jax.shard_map(local, mesh=mesh, in_specs=in_specs, out_specs=both, check_vma=False)
```

```python
import functools
import jax
import jax.numpy as jnp
import numpy as np
from jax import lax
from jax.experimental import pallas as pl
from jax.experimental.pallas import tpu as pltpu
from jax.sharding import PartitionSpec as P

GROUPS = 32
LAT_W = 32
SKIP = 320
DEEP = 640
WIDTH = SKIP + DEEP
OUT = 320
MAIN = 256
REST = OUT - MAIN
RANK = 64
CHUNK = 256
MESH = pl.DeviceIdType.MESH
def same_group():
    ids = np.arange(WIDTH) // (WIDTH // GROUPS)
    return (ids[:, None] == ids[None, :]).astype(np.float32)


def dot_t(a, b):
    return lax.dot_general(a, b, (((1,), (1,)), ((), ())), preferred_element_type=jnp.float32)


def flip(value, mask, count):
    out, bit = 0, 1
    while bit < count:
        mine = (value // bit) % 2
        out = out + bit * ((1 - mine) if mask & bit else mine)
        bit *= 2
    return out


def group_sum(v, same):
    v = jnp.sum(v, axis=0, keepdims=True)
    hi = v.astype(jnp.bfloat16).astype(jnp.float32)
    mid = (v - hi).astype(jnp.bfloat16).astype(jnp.float32)
    lo = v - hi - mid
    r = lax.broadcasted_iota(jnp.int32, (16, v.shape[1]), 0)
    rows = jnp.where(r == 0, hi, jnp.where(r == 1, mid, jnp.where(r == 2, lo, 0.0))).astype(jnp.bfloat16)
    return jnp.sum(jnp.dot(rows, same, preferred_element_type=jnp.float32), axis=0, keepdims=True)


def kernel(B, L, tp, req, lib, cached_h, down, up, skip_h, kw_h, sc_h, gain, offset, bias, same_h, out,
           cached, send, deep, ids, dall, uall, w, sc, skip_t, skip, x, y, acc, same,
           s_send, s_recv, z_send, z_recv, f_send, f_recv, l_sem, w_sem):
    b, l = lax.axis_index("batch"), lax.axis_index("lib")
    column, block = cached.shape[0], cached.shape[1]
    per, places = deep.shape[0], deep.shape[1]
    n = down.shape[0]
    h = n // 2
    half = b % 2
    peers = [flip(b, d, B) for d in range(B - 1, 0, -1)]
    zpeers = [(l + d) % L for d in range(1, L)]
    sib = peers[-1]

    load_cached = pltpu.make_async_copy(cached_h, cached, l_sem.at[0])
    load_cached.start()
    loads = [
        pltpu.make_async_copy(skip_h, skip_t, l_sem.at[1]),
        pltpu.make_async_copy(sc_h, sc, l_sem.at[2]),
        pltpu.make_async_copy(same_h, same, l_sem.at[3]),
    ]
    w_loads = []
    for dr in range(3):
        for dc in range(3):
            i = 2 * (3 * dr + dc)
            w_loads.append(pltpu.make_async_copy(
                kw_h.at[dr, dc, pl.ds(0, MAIN)], w.at[dc, pl.ds(dr * MAIN, MAIN)], w_sem.at[i]))
            w_loads.append(pltpu.make_async_copy(
                kw_h.at[dr, dc, pl.ds(MAIN, REST)], w.at[dc, pl.ds(3 * MAIN + dr * REST, REST)], w_sem.at[i + 1]))

    barrier = pltpu.get_barrier_semaphore()
    for p in peers:
        pl.semaphore_signal(barrier, inc=1, device_id=(p, l), device_id_type=MESH)
    for z in zpeers:
        pl.semaphore_signal(barrier, inc=1, device_id=(b, z), device_id_type=MESH)
    pl.semaphore_wait(barrier, len(peers) + len(zpeers))

    def to_peer(s, p, src):
        return pltpu.make_async_remote_copy(
            src_ref=send.at[p * per + s], dst_ref=deep.at[s, pl.ds(pl.multiple_of(src * block, block), block)],
            send_sem=s_send.at[s, p], recv_sem=s_recv.at[s, src],
            device_id=(p, l), device_id_type=MESH)

    def slot(t):
        j = jnp.int32(0)
        for i in range(column):
            j = jnp.where(tp[0, i] == t, i, j)
        return j

    def inside(v):
        return jnp.logical_and(v >= 0, v < L)

    def z_copies(way, src):
        row = pl.ds(src * n + half * h, h)
        kw = dict(device_id=(b, (l + way + L) % L), device_id_type=MESH)
        return [
            pltpu.make_async_remote_copy(src_ref=ref, dst_ref=ref, send_sem=z_send.at[i, (way + 1) // 2, src],
                                         recv_sem=z_recv.at[i, src], **kw)
            for i, ref in enumerate((ids.at[src], dall.at[row], uall.at[row]))
        ]

    def pass_on(way, src, done=False):
        @pl.when(inside(l + way))
        def _():
            for c in z_copies(way, src):
                c.wait_send() if done else c.start()

    def f_copies(src, side):
        row = pl.ds(src * n + side * h, h)
        kw = dict(device_id=(sib, l), device_id_type=MESH)
        return [
            pltpu.make_async_remote_copy(src_ref=dall.at[row], dst_ref=dall.at[row],
                                         send_sem=f_send.at[0, src], recv_sem=f_recv.at[0, src], **kw),
            pltpu.make_async_remote_copy(src_ref=uall.at[row], dst_ref=uall.at[row],
                                         send_sem=f_send.at[1, src], recv_sem=f_recv.at[1, src], **kw),
        ]

    def z_step(d):
        for way in (1, -1):
            src = l - way * d

            @pl.when(inside(src))
            def _():
                for c in z_copies(way, src):
                    c.wait_recv()
                pass_on(way, src)
                for c in f_copies(src, half):
                    c.start()

    def z_sent(d):
        for way in (1, -1):
            src = l - way * d

            @pl.when(inside(src))
            def _():
                pass_on(way, src, done=True)

    dall[pl.ds(l * n, n)] = down[...]
    uall[pl.ds(l * n, n)] = up[...]
    row_id = lax.broadcasted_iota(jnp.int32, ids.shape[1:], 0)
    mine = jnp.full(ids.shape[1:], -1, jnp.int32)
    for i in range(n):
        mine = jnp.where(row_id == i, lib[i], mine)
    ids[l] = mine
    for way in (1, -1):
        pass_on(way, l)
    load_cached.wait()
    for s in range(per):
        for p in peers:
            send[p * per + s] = cached[slot(p * per + s)]
            if s == 0:
                to_peer(s, p, b).start()
    for c in loads + w_loads:
        c.start()
    for s in range(per):
        deep[s, pl.ds(pl.multiple_of(b * block, block), block), :] = cached[slot(b * per + s)]
    edge = jnp.zeros((3, LAT_W, 1024), jnp.float32)
    y[:, :LAT_W, :] = edge
    y[:, places + LAT_W:, :] = edge
    for c in loads:
        c.wait()

    for s in range(per):
        for i in range(places // CHUNK):
            at = pl.ds(i * CHUNK, CHUNK)
            sk = skip_t[s, :, at].astype(jnp.float32).T.astype(jnp.bfloat16)
            skip[s, at, :] = sk
            acc[s, at, :] = dot_t(sk, sc[:, :SKIP]) + bias[...]
        if s + 1 < L - 1:
            z_step(s + 1)

    for s in range(1, per):
        for p in peers:
            to_peer(s - 1, p, b).wait_send()
            to_peer(s, p, b).start()
    for c in w_loads:
        c.wait()
    number = lax.broadcasted_iota(jnp.int32, ids.shape, 0) * n + lax.broadcasted_iota(jnp.int32, ids.shape, 1)
    count = places * (WIDTH // GROUPS)
    step = 256

    def request(s, carry):
        for p in peers:
            to_peer(s, p, p).wait_recv()

        def both(i):
            at = pl.ds(pl.multiple_of(i * step, step), step)
            return skip[s, at, :].astype(jnp.float32), deep[s, at, :].astype(jnp.float32)

        def fold(v):
            return jnp.sum(v.reshape(step // 8, 8, v.shape[1]), axis=0)

        def total(i, c):
            a, d = both(i)
            return c[0] + fold(a), c[1] + fold(d)

        zero = (jnp.zeros((8, SKIP), jnp.float32), jnp.zeros((8, DEEP), jnp.float32))
        t = lax.fori_loop(0, places // step, total, zero)
        mean = group_sum(jnp.concatenate(t, axis=1), same[...]) * (1.0 / count)
        mean_s, mean_d = mean[:, :SKIP], mean[:, SKIP:]

        def square(i, c):
            a, d = both(i)
            a, d = a - mean_s, d - mean_d
            return c[0] + fold(a * a), c[1] + fold(d * d)

        t = lax.fori_loop(0, places // step, square, zero)
        var = group_sum(jnp.concatenate(t, axis=1), same[...]) * (1.0 / count)
        scale = 0.5 * gain[...] * lax.rsqrt(var + 1e-5)
        shift = 0.5 * offset[...]
        scale_s, scale_d = scale[:, :SKIP], scale[:, SKIP:]
        shift_s, shift_d = shift[:, :SKIP], shift[:, SKIP:]

        def normed(i, c):
            a, d = both(i)
            a = (a - mean_s) * scale_s + shift_s
            d = (d - mean_d) * scale_d + shift_d
            a = (a + a * jnp.tanh(a)).astype(jnp.bfloat16)
            d = (d + d * jnp.tanh(d)).astype(jnp.bfloat16)
            x[pl.ds(pl.multiple_of(i * step, step), step), :] = jnp.concatenate([a, d], axis=1)
            return c

        lax.fori_loop(0, places // step, normed, 0)

        @pl.when(s == 0)
        def _():
            for d in range(min(per, L - 2) + 1, L):
                z_step(d)
            for z in zpeers:
                for c in f_copies(z, 1 - half):
                    c.wait_recv()

        k = jnp.max(jnp.where(ids[...] == req[s], number, 0))
        w[1, 3 * OUT:, :] = dall[k]
        u = uall[k]

        def conv(i, c):
            p = pl.multiple_of(i * CHUNK, CHUNK)
            at = pl.ds(p, CHUNK)
            xs = x[at, :]
            to = pl.ds(pl.multiple_of(p + LAT_W, LAT_W), CHUNK)
            y1 = dot_t(xs, w[1])
            y[1, to, :] = y1
            y[0, to, :3 * OUT] = dot_t(xs, w[0, :3 * OUT])
            y[2, to, :3 * OUT] = dot_t(xs, w[2, :3 * OUT])
            acc[s, at, :] += (
                dot_t(deep[s, at, :], sc[:, SKIP:])
                + jnp.dot(y1[:, 3 * OUT:].astype(jnp.bfloat16), u, preferred_element_type=jnp.float32)
            )
            return c

        lax.fori_loop(0, places // CHUNK, conv, 0)
        side = 128

        def gather_taps(i, c):
            p = pl.multiple_of(i * side, side)
            col = lax.broadcasted_iota(jnp.int32, (side, 1), 0) % LAT_W

            def rows(dc, dr, lo, size):
                return y[dc, pl.ds(pl.multiple_of(p + dr * LAT_W, LAT_W), side), lo:lo + size]

            def column_sum(dc):
                a = rows(dc, 0, 0, MAIN) + rows(dc, 1, MAIN, MAIN) + rows(dc, 2, 2 * MAIN, MAIN)
                e = (rows(dc, 0, 3 * MAIN, 128) + rows(dc, 2, 3 * MAIN + 128, 128))[:, :REST]
                e = e + rows(dc, 1, 3 * MAIN, 128)[:, REST:]
                return jnp.concatenate([a, e], axis=1)

            v = column_sum(1) + acc[s, pl.ds(p, side), :]
            v = v + jnp.where(col != 0, pltpu.roll(column_sum(0), 1, 0), 0.0)
            v = v + jnp.where(col != LAT_W - 1, pltpu.roll(column_sum(2), side - 1, 0), 0.0)
            out[s, :, pl.ds(p, side)] = v.T.astype(jnp.bfloat16)
            return c

        lax.fori_loop(0, places // side, gather_taps, 0)
        return carry

    lax.fori_loop(0, per, request, 0)
    for d in range(L):
        z_sent(d)
    for z in zpeers:
        for c in f_copies(z, half):
            c.wait_send()
    for p in peers:
        to_peer(per - 1, p, b).wait_send()


def solution(mesh):
    B, L = mesh.shape["batch"], mesh.shape["lib"]

    def local(skip, cached, tp, req, lib, down, up, kw, sc, gain, offset, bias):
        per, places = skip.shape[0], skip.shape[1]
        n, column, block = down.shape[0], cached.shape[0], cached.shape[1]
        vm = pl.BlockSpec(memory_space=pltpu.VMEM)
        sm = pl.BlockSpec(memory_space=pltpu.SMEM)
        hbm = pl.BlockSpec(memory_space=pl.ANY)
        dma = pltpu.SemaphoreType.DMA
        bf, f32 = jnp.bfloat16, jnp.float32
        out = pl.pallas_call(
            functools.partial(kernel, B, L),
            out_shape=jax.ShapeDtypeStruct((per, OUT, places), bf),
            in_specs=[sm, sm, sm, hbm, vm, vm, hbm, hbm, hbm, vm, vm, vm, hbm],
            out_specs=vm,
            scratch_shapes=[
                pltpu.VMEM((column, block, DEEP), bf),
                pltpu.VMEM((column, block, DEEP), bf),
                pltpu.VMEM((per, places, DEEP), bf),
                pltpu.VMEM((L, 8 * ((n + 7) // 8), 128), jnp.int32),
                pltpu.VMEM((L * n, RANK, WIDTH), bf),
                pltpu.VMEM((L * n, RANK, OUT), bf),
                pltpu.VMEM((3, 1024, WIDTH), bf),
                pltpu.VMEM((OUT, WIDTH), bf),
                pltpu.VMEM((per, SKIP, places), bf),
                pltpu.VMEM((per, places, SKIP), bf),
                pltpu.VMEM((places, WIDTH), bf),
                pltpu.VMEM((3, places + 2 * LAT_W, 1024), f32),
                pltpu.VMEM((per, places, OUT), f32),
                pltpu.VMEM((WIDTH, WIDTH), bf),
                dma((per, B)), dma((per, B)), dma((3, 2, L)), dma((3, L)), dma((2, L)), dma((2, L)), dma((4,)),
                dma((18,)),
            ],
            compiler_params=pltpu.CompilerParams(
                collective_id=0, has_side_effects=True, vmem_limit_bytes=60 * 1024 * 1024),
        )(tp, req, lib, cached, down, up, skip.transpose(0, 2, 1), kw.transpose(0, 1, 3, 2), sc.T,
          gain[None], offset[None], bias[None], jnp.asarray(same_group(), bf))
        return out.transpose(0, 2, 1)

    both = P(("batch", "lib"), None, None)
    lib3 = P("lib", None, None)
    in_specs = (both, P("lib", "batch", None), P("lib", None), P(("batch", "lib")), P("lib"), lib3, lib3,
                P(), P(), P(), P(), P())
    return jax.shard_map(local, mesh=mesh, in_specs=in_specs, out_specs=both, check_vma=False)
```
